32 devices in a mesh: row: 8 (over z, core), col: 4 (over y, x).
Axes of the slice: x: 2, y: 2, z: 4, core: 2. Of those that a mesh axis runs over, the one named last changes fastest.
Arguments:
- chars: bfloat16 [512, 8192], P(('row', 'col')), may hold values from -6 to 6
- pool_weight: bfloat16 [32768, 8192], P('col', 'row'), may hold values from -0.5 to 0.5
- gain_attn: bfloat16 [8192], P('row'), may hold values from 0.099609375 to 1.8984375
- w_query: bfloat16 [8192, 8192], P('row', 'col'), may hold values from -0.5 to 0.5
- w_key: bfloat16 [8192, 8192], P('row', 'col'), may hold values from -3 to 3
- w_value: bfloat16 [8192, 8192], P('row', 'col'), may hold values from -0.0625 to 0.0625
- w_out: bfloat16 [8192, 8192], P('col', 'row'), may hold values from -0.0625 to 0.0625
- gain_ffn: bfloat16 [8192], P('row'), may hold values from 0.099609375 to 1.8984375
- w_gate: bfloat16 [8192, 28672], P('row', 'col'), may hold values from -0.0625 to 0.0625
- w_up: bfloat16 [8192, 28672], P('row', 'col'), may hold values from -0.0625 to 0.0625
- w_down: bfloat16 [28672, 8192], P('col', 'row'), may hold values from -0.03125 to 0.03125
Outputs:
- upsampled: bfloat16 [512, 8192], P(('row', 'col'))
The draws below stay inside these ranges and needn't reach their ends.
All inputs are finite; a program needn't handle non-finite values.
Results may differ from the reference program's by a relative error of at most 0.02.
Values may be sent and summed in bfloat16 or wider, within the bound.
A program may use at most 256 MiB of HBM per device.

```python
import jax
import jax.numpy as jnp
from jax import lax

D = 8192
FF = 28672
HD = 128
POOL = 4
CHARS = 512
TOKENS = 128
N_ROW = 8
N_COL = 4


def shared_weight(key):
    return jnp.clip(jax.random.normal(key, (D, D), jnp.float32), -6.0, 6.0) * D ** (-0.5)


def column_rise(low, high):
    places = jnp.arange(D, dtype=jnp.float32) / jnp.float32(D - 1)
    return jnp.exp(jnp.log(jnp.float32(low)) + jnp.log(jnp.float32(high / low)) * places)


def draw_pool_weight(key, part):
    key = jax.random.fold_in(key, 37)
    entries = jnp.clip(jax.random.normal(key, (POOL * D, D), jnp.float32), -6.0, 6.0) * (POOL * D) ** (-0.5)
    scales = column_rise(0.5, 2.0)
    return (entries * scales[None, :]).astype(jnp.bfloat16)


def draw_w_query(key, part):
    common = shared_weight(key)
    return common.astype(jnp.bfloat16)


def draw_w_key(key, part):
    key = jax.random.fold_in(key, 23)
    fresh = jnp.clip(jax.random.normal(key, (D, D), jnp.float32), -6.0, 6.0) * D ** (-0.5)
    result = fresh
    return result.astype(jnp.bfloat16)


def steps_of(stream_key, dims, split, least, largest):
    level, own = 1.0, jax.random.fold_in(stream_key, 6)
    for axis_at, blocks in split:
        draws = jnp.exp(jax.random.uniform(jax.random.fold_in(own, axis_at), (blocks,), jnp.float32, least / len(split), largest / len(split)))
        level = level * jnp.repeat(draws, dims[axis_at] // blocks).reshape([-1 if axis == axis_at else 1 for axis in range(len(dims))])
    return level


def centred(rng, extent, deviation, most, cuts=(), held_as=jnp.bfloat16):
    array = deviation * jax.random.normal(rng, extent, jnp.float32)
    if cuts:
        array = array * steps_of(rng, extent, cuts, -0.22, 0.18)
    return jnp.clip(array, -most, most).astype(held_as)


def setup_inputs(seed: int = 0) -> dict:
    keys = jax.random.split(jax.random.key(seed), 12)
    chars = centred(keys[0], (CHARS, D), 1.0, 6.0, ((0, 32),))
    pool_weight = draw_pool_weight(jax.random.fold_in(keys[11], 71), 0)
    gain_attn = jnp.clip(1.0 + 0.18 * jax.random.normal(keys[2], (D,), jnp.float32), 0.099609375, 1.8984375).astype(jnp.bfloat16)
    w_query = draw_w_query(jax.random.fold_in(keys[11], 71), 0)
    w_key = draw_w_key(jax.random.fold_in(keys[11], 71), 0)
    w_value = centred(keys[5], (D, D), D ** -0.5, 0.0625, ((0, 8), (1, 4)))
    w_out = centred(keys[6], (D, D), D ** -0.5, 0.0625, ((0, 4), (1, 8)))
    gain_ffn = jnp.clip(1.0 + 0.18 * jax.random.normal(keys[7], (D,), jnp.float32), 0.099609375, 1.8984375).astype(jnp.bfloat16)
    w_gate = centred(keys[8], (D, FF), D ** -0.5, 0.0625, ((0, 8), (1, 4)))
    w_up = centred(keys[9], (D, FF), D ** -0.5, 0.0625, ((0, 8), (1, 4)))
    w_down = centred(keys[10], (FF, D), FF ** -0.5, 0.03125, ((0, 4), (1, 8)))
    return dict(chars=chars, pool_weight=pool_weight, gain_attn=gain_attn, w_query=w_query, w_key=w_key, w_value=w_value, w_out=w_out, gain_ffn=gain_ffn, w_gate=w_gate, w_up=w_up, w_down=w_down)


EPS = 1e-05

def block_sum(left, right, parts):
    width = left.shape[1] // parts
    total = jnp.zeros((left.shape[0], right.shape[1]), jnp.float32)
    for block in range(parts):
        term = jnp.dot(left[:, block * width:(block + 1) * width], right[block * width:(block + 1) * width], preferred_element_type=jnp.float32)
        total = total + lax.optimization_barrier(term.astype(jnp.bfloat16)).astype(jnp.float32)
    return total

def rms_normed(hidden, gain):
    values = hidden.astype(jnp.float32)
    factor = lax.rsqrt(lax.optimization_barrier(jnp.mean(values * values, axis=-1, keepdims=True)) + EPS)
    return (values * factor * gain.astype(jnp.float32)).astype(jnp.bfloat16)

def attention(queries, keys_part, values_part):
    length = queries.shape[0]
    query_heads = queries.reshape(length, -1, HD).astype(jnp.float32)
    key_heads = keys_part.reshape(length, -1, HD).astype(jnp.float32)
    value_heads = values_part.reshape(length, -1, HD).astype(jnp.float32)
    scores = jnp.einsum('qhd,khd->hqk', query_heads, key_heads) * HD ** (-0.5)
    positions = jnp.arange(length, dtype=jnp.int32)
    allowed = positions[:, None] >= positions[None, :]
    scores = jnp.where(allowed[None], scores, jnp.float32(-1e+30))
    highest = lax.optimization_barrier(jnp.max(scores, axis=-1, keepdims=True))
    weights = jnp.exp(scores - highest)
    weights = (weights / lax.optimization_barrier(jnp.sum(weights, axis=-1, keepdims=True))).astype(jnp.bfloat16)
    mixed = jnp.einsum('hqk,khd->qhd', weights.astype(jnp.float32), value_heads)
    return mixed.astype(jnp.bfloat16).reshape(length, -1)

def reference(chars, pool_weight, gain_attn, w_query, w_key, w_value, w_out, gain_ffn, w_gate, w_up, w_down):
    grouped = chars.reshape(TOKENS, POOL * D)
    pooled = block_sum(grouped, pool_weight, N_COL).astype(jnp.bfloat16)
    normed_attn = rms_normed(pooled, gain_attn)
    queries = block_sum(normed_attn, w_query, N_ROW).astype(jnp.bfloat16)
    keys_part = block_sum(normed_attn, w_key, N_ROW).astype(jnp.bfloat16)
    values_part = block_sum(normed_attn, w_value, N_ROW).astype(jnp.bfloat16)
    mixed = attention(queries, keys_part, values_part)
    first = (pooled.astype(jnp.float32) + block_sum(mixed, w_out, N_COL)).astype(jnp.bfloat16)
    normed_ffn = rms_normed(first, gain_ffn)
    gate = block_sum(normed_ffn, w_gate, N_ROW)
    upward = block_sum(normed_ffn, w_up, N_ROW)
    activated = (jax.nn.silu(gate) * upward).astype(jnp.bfloat16)
    second = (first.astype(jnp.float32) + block_sum(activated, w_down, N_COL)).astype(jnp.bfloat16)
    expanded = jnp.repeat(second, POOL, axis=0)
    return (chars.astype(jnp.float32) + expanded.astype(jnp.float32)).astype(jnp.bfloat16)
```

```python
import functools

import jax
import jax.numpy as jnp
from jax import lax
from jax.experimental import pallas as pl
from jax.experimental.pallas import tpu as pltpu
from jax.sharding import PartitionSpec as P

D = 8192
HD = 128
POOL = 4


EPS = 1e-05


def square_sum(hidden):
    values = hidden.astype(jnp.float32)
    return jnp.sum(values * values, axis=-1)


def norm_apply(hidden, totals, gain):
    factor = lax.rsqrt(totals / D + EPS)[..., None]
    return (hidden.astype(jnp.float32) * factor * gain.astype(jnp.float32)).astype(jnp.bfloat16)


def attend(queries, keys_part, values_part, offset):
    query_count = queries.shape[0]
    key_count = keys_part.shape[0]
    query_heads = queries.reshape(query_count, -1, HD)
    key_heads = keys_part.reshape(key_count, -1, HD)
    value_heads = values_part.reshape(key_count, -1, HD)
    scores = jnp.einsum(
        "qhd,khd->hqk", query_heads, key_heads, preferred_element_type=jnp.float32
    ) * HD ** (-0.5)
    query_places = offset + jnp.arange(query_count, dtype=jnp.int32)
    key_places = jnp.arange(key_count, dtype=jnp.int32)
    allowed = query_places[:, None] >= key_places[None, :]
    scores = jnp.where(allowed[None], scores, jnp.float32(-1e30))
    highest = jnp.max(scores, axis=-1, keepdims=True)
    weights = jnp.exp(scores - highest)
    weights = (weights / jnp.sum(weights, axis=-1, keepdims=True)).astype(jnp.bfloat16)
    mixed = jnp.einsum("hqk,khd->qhd", weights, value_heads, preferred_element_type=jnp.float32)
    return mixed.astype(jnp.bfloat16).reshape(query_count, -1)


def by_collectives(
    chars, pool_weight, gain_attn, w_query, w_key, w_value, w_out, gain_ffn, w_gate, w_up, w_down
):
    rows_count = lax.axis_size("row")
    cols_count = lax.axis_size("col")
    char_rows = chars.shape[0]
    tokens_here = char_rows // POOL
    feature_block = pool_weight.shape[1]
    grouped = chars.reshape(1, 1, tokens_here, POOL * chars.shape[1])
    spread = lax.all_to_all(grouped, "col", split_axis=3, concat_axis=1, tiled=True)
    piece = lax.all_gather(spread, "row", axis=0, tiled=True)
    pool_terms = jnp.dot(
        piece.reshape(-1, piece.shape[3]), pool_weight, preferred_element_type=jnp.float32
    )
    pool_terms = pool_terms.reshape(rows_count, cols_count, tokens_here, feature_block)
    pooled = lax.psum_scatter(
        pool_terms.astype(jnp.bfloat16), "col", scatter_dimension=1, tiled=True
    )
    attn_totals = lax.psum(square_sum(pooled), "row")
    normed_attn = norm_apply(pooled, attn_totals, gain_attn)
    gathered = lax.all_gather(normed_attn, "col", axis=1, tiled=True).reshape(-1, feature_block)
    seq_length = gathered.shape[0]
    block_rows = seq_length // rows_count
    slab = gathered
    queries = lax.psum_scatter(
        jnp.dot(slab, w_query, preferred_element_type=jnp.float32).astype(jnp.bfloat16),
        "row",
        scatter_dimension=0,
        tiled=True,
    )
    slab = gathered
    pair_local = lax.psum_scatter(
        jnp.concatenate(
            [
                jnp.dot(slab, w_key, preferred_element_type=jnp.float32),
                jnp.dot(slab, w_value, preferred_element_type=jnp.float32),
            ],
            axis=1,
        ).astype(jnp.bfloat16),
        "row",
        scatter_dimension=0,
        tiled=True,
    )
    pair_whole = lax.all_gather(pair_local, "row", axis=0, tiled=True)
    head_columns = w_query.shape[1]
    keys_part = pair_whole[:, :head_columns]
    values_part = pair_whole[:, head_columns:]
    mixed = attend(queries, keys_part, values_part, lax.axis_index("row") * block_rows)
    out_terms = jnp.dot(
        lax.all_gather(mixed, "row", axis=0, tiled=True), w_out, preferred_element_type=jnp.float32
    )
    out_terms = out_terms.reshape(rows_count, cols_count, tokens_here, feature_block)
    attn_total = lax.psum_scatter(
        out_terms.astype(jnp.bfloat16), "col", scatter_dimension=1, tiled=True
    ).astype(jnp.float32)
    first = (pooled.astype(jnp.float32) + attn_total).astype(jnp.bfloat16)
    ffn_totals = lax.psum(square_sum(first), "row")
    normed_ffn = norm_apply(first, ffn_totals, gain_ffn)
    gathered_ffn = lax.all_gather(normed_ffn, "col", axis=1, tiled=True).reshape(-1, feature_block)
    hidden_local = w_gate.shape[1]
    slab = gathered_ffn
    hidden_pair = lax.psum_scatter(
        jnp.concatenate(
            [
                jnp.dot(slab, w_gate, preferred_element_type=jnp.float32),
                jnp.dot(slab, w_up, preferred_element_type=jnp.float32),
            ],
            axis=1,
        ).astype(jnp.bfloat16),
        "row",
        scatter_dimension=0,
        tiled=True,
    ).astype(jnp.float32)
    activated = (jax.nn.silu(hidden_pair[:, :hidden_local]) * hidden_pair[:, hidden_local:]).astype(
        jnp.bfloat16
    )
    down_terms = jnp.dot(
        lax.all_gather(activated, "row", axis=0, tiled=True),
        w_down,
        preferred_element_type=jnp.float32,
    )
    down_terms = down_terms.reshape(rows_count, cols_count, tokens_here, feature_block)
    ffn_total = lax.psum_scatter(
        down_terms.astype(jnp.bfloat16), "col", scatter_dimension=1, tiled=True
    ).astype(jnp.float32)
    second = (first.astype(jnp.float32) + ffn_total).astype(jnp.bfloat16)
    returned = lax.all_to_all(second, "row", split_axis=0, concat_axis=3, tiled=True)
    expanded = jnp.repeat(returned.reshape(tokens_here, -1), POOL, axis=0)
    return (chars.astype(jnp.float32) + expanded.astype(jnp.float32)).astype(jnp.bfloat16)


MESH = pl.DeviceIdType.MESH
BF = jnp.bfloat16
F32 = jnp.float32
SLOTS = 20
SUB = 16


def one_hot(shape, test):
    rows_at = lax.broadcasted_iota(jnp.int32, shape, 0)
    cols_at = lax.broadcasted_iota(jnp.int32, shape, 1)
    return jnp.where(test(rows_at, cols_at), 1.0, 0.0).astype(BF)


def mm(left, right):
    return jnp.dot(left, right, preferred_element_type=F32)


def layer_kernel(
    sizes, chars, pool_w, gain_a, wq, wk, wv, wo, gain_f, wg, wu, wd, out,
    ring, ring_sem,
    stage, xin, xall, part, crecv, hall, scaled, resid,
    sq, sqrecv, factor,
    qp, qsib, qsum, qz, mixall,
    gp, gsib, gsum, gz, act, dacc,
    fsend, frecv,
    a2a_s, a2a_r, xz_s, xz_r, xs_s, xs_r, rs_s, rs_r, ag_s, ag_r, sq_s, sq_r,
    qs_s, qs_r, qz_s, qz_r, mz_s, mz_r, ms_s, ms_r,
    gs_s, gs_r, gz_s, gz_r, az_s, az_r, as_s, as_r, fin_s, fin_r,
):
    rows, cols, tokens, width, here, chunks = sizes
    deep = rows // 2
    quarter = SUB // here
    piece = chars.shape[1] // quarter
    share = tokens // cols
    mine = tokens // rows
    half = tokens // 2
    head_cols = wq.shape[1] // rows
    tile = head_cols
    row = lax.axis_index("row")
    col = lax.axis_index("col")
    level = lax.div(row, 2)
    core = lax.rem(row, 2)
    other = 1 - core
    sibling = (level * 2 + other, col)
    pending = []

    def send(source, target, s_sem, r_sem, where):
        copy = pltpu.make_async_remote_copy(
            src_ref=source, dst_ref=target, send_sem=s_sem, recv_sem=r_sem,
            device_id=where, device_id_type=MESH,
        )
        copy.start()
        pending.append(copy)
        return copy

    def col_at(d):
        return lax.rem(col + d, cols)

    def level_at(d):
        return lax.rem(level + d, deep)

    def row_at(d):
        return lax.rem(row + d, rows)

    blocks = [(pool_w, i, 0) for i in range(pool_w.shape[0] // width)]
    n_pool = len(blocks)
    for weight in (wq, wk, wv):
        blocks += [(weight, 0, i) for i in range(weight.shape[1] // width)]
    n_qkv = len(blocks)
    blocks += [(wo, i, 0) for i in range(wo.shape[0] // width)]
    n_out = len(blocks)
    for i in range(chunks):
        blocks += [(wg, 0, i), (wu, 0, i)]
    n_up = len(blocks)
    blocks += [(wd, i, 0) for i in range(chunks)]

    def fetch(i):
        ref, down, across = blocks[i]
        return pltpu.make_async_copy(
            ref.at[pl.ds(down * width, width), pl.ds(across * width, width)],
            ring.at[i % SLOTS], ring_sem.at[i],
        )

    def fetch_after(first, last):
        for i in range(first, last):
            if i + SLOTS < len(blocks):
                fetch(i + SLOTS).start()

    for i in range(min(SLOTS, len(blocks))):
        fetch(i).start()

    barrier = pltpu.get_barrier_semaphore()
    for d in range(1, cols):
        pl.semaphore_signal(barrier, inc=1, device_id=(row, col_at(d)), device_id_type=MESH)
    for d in range(1, rows):
        pl.semaphore_signal(barrier, inc=1, device_id=(row_at(d), col), device_id_type=MESH)

    for q in range(quarter):
        pick = one_hot(
            (cols * SUB, here * cols),
            lambda i, m: (m == (i % here) * cols + i // SUB) & ((i % SUB) // here == q),
        )
        term = mm(pick, chars[:, q * piece:(q + 1) * piece])
        if q == 0:
            total = term
        else:
            total = total + term
    stage[...] = total.astype(BF)
    at = pl.multiple_of(col * SUB, SUB)
    xin[pl.ds(at, SUB), :] = stage[pl.ds(at, SUB), :]
    pl.semaphore_wait(barrier, cols + rows - 2)
    copies = []
    for d in range(1, cols):
        copies.append(send(
            stage.at[pl.ds(pl.multiple_of(col_at(d) * SUB, SUB), SUB), :], xin.at[pl.ds(at, SUB), :],
            a2a_s.at[d], a2a_r.at[d], (row, col_at(d)),
        ))
    for copy in copies:
        copy.wait_recv()
    here_at = pl.multiple_of(row * mine, mine)
    for q in range(quarter):
        pick = one_hot(
            (mine, cols * SUB),
            lambda i, m: (m // SUB == i // here) & (m % here == i % here) & ((m % SUB) // here == q),
        )
        xall[pl.ds(here_at, mine), q * piece:(q + 1) * piece] = mm(pick, xin[...]).astype(BF)

    def x_rows(level_of, core_of):
        return xall.at[pl.ds(pl.multiple_of((level_of * 2 + core_of) * mine, mine), mine), :]

    copies = []
    for d in range(1, deep):
        copies.append(send(
            x_rows(level, core), x_rows(level, core), xz_s.at[d], xz_r.at[d], (level_at(d) * 2 + core, col),
        ))
    sibs = [send(x_rows(level, core), x_rows(level, core), xs_s.at[0], xs_r.at[0], sibling)]
    for d in range(1, deep):
        copies[d - 1].wait_recv()
        source = level_at(deep - d)
        sibs.append(send(x_rows(source, core), x_rows(source, core), xs_s.at[d], xs_r.at[d], sibling))
    for copy in sibs:
        copy.wait_recv()

    for i in range(n_pool):
        fetch(i).wait()
    order = one_hot(
        (tokens, tokens),
        lambda i, m: m == ((i % share) // here) * mine + (i // share) * here + i % here,
    )

    @pl.loop(0, width // tile)
    def _(n):
        across = pl.ds(pl.multiple_of(n * tile, tile), tile)
        total = jnp.zeros((tokens, tile), F32)
        for i in range(n_pool):
            total = total + mm(xall[:, i * width:(i + 1) * width], ring[i % SLOTS, :, across])
        part[0, :, across] = mm(order, total.astype(BF)).astype(BF)

    fetch_after(0, n_pool)
    share_at = pl.multiple_of(col * share, share)
    my_share = pl.ds(share_at, share)

    def reduce_cols(step):
        copies = []
        for d in range(1, cols):
            copies.append(send(
                part.at[step, pl.ds(pl.multiple_of(col_at(d) * share, share), share), :],
                crecv.at[step, d - 1], rs_s.at[step, d], rs_r.at[step, d], (row, col_at(d)),
            ))
        for copy in copies:
            copy.wait_recv()
        total = part[step, my_share, :].astype(F32)
        for d in range(1, cols):
            total = total + crecv[step, d - 1].astype(F32)
        return total

    def spread_norm(step, values, gain):
        resid[...] = values
        hall[step, my_share, :] = values
        copies = []
        for d in range(1, cols):
            copies.append(send(
                hall.at[step, my_share, :], hall.at[step, my_share, :],
                ag_s.at[step, d], ag_r.at[step, d], (row, col_at(d)),
            ))
        for copy in copies:
            copy.wait_recv()
        whole = hall[step].astype(F32)
        scaled[...] = (whole * gain[...].astype(F32)).astype(BF)
        squares = jnp.sum(whole * whole, axis=1, keepdims=True)
        flat = jnp.broadcast_to(squares, (tokens, tokens)).T
        sq[step] = flat[:8]
        return [
            send(sq.at[step], sqrecv.at[step, d - 1], sq_s.at[step, d], sq_r.at[step, d], (row_at(d), col))
            for d in range(1, rows)
        ]

    def take_factor(step, copies):
        for copy in copies:
            copy.wait_recv()
        total = sq[step]
        for d in range(1, rows):
            total = total + sqrecv[step, d - 1]
        line = lax.rsqrt(total / (rows * width) + EPS)
        factor[...] = jnp.broadcast_to(line[:1], (tokens, tokens)).T

    sq_copies = spread_norm(0, reduce_cols(0).astype(BF), gain_a)

    per = width // tile
    for kind in range(3):
        for b in range(wq.shape[1] // width):
            i = n_pool + kind * (wq.shape[1] // width) + b
            fetch(i).wait()

            @pl.loop(0, per)
            def _(n):
                owner = b * per + n
                across = pl.ds(pl.multiple_of(n * tile, tile), tile)
                qp[lax.rem(owner, 2), lax.div(owner, 2), :, kind * tile:(kind + 1) * tile] = mm(
                    scaled[...], ring[i % SLOTS, :, across]
                ).astype(BF)

    fetch_after(n_pool, n_qkv)
    send(qp.at[other], qsib, qs_s, qs_r, sibling).wait_recv()
    copies = []
    for d in list(range(1, deep)) + [0]:
        there = level_at(d)
        qsum[there] = (qp[core, there].astype(F32) + qsib[there].astype(F32)).astype(BF)
        if d:
            copies.append(send(
                qsum.at[there], qz.at[d - 1], qz_s.at[d], qz_r.at[d], (there * 2 + core, col)
            ))
    take_factor(0, sq_copies)
    for copy in copies:
        copy.wait_recv()
    places_i = lax.broadcasted_iota(jnp.int32, (tokens, tokens), 0)
    places_j = lax.broadcasted_iota(jnp.int32, (tokens, tokens), 1)

    def true_place(i):
        return ((i % share) // here) * mine + (i // share) * here + i % here

    allowed = true_place(places_i) >= true_place(places_j)

    def head_part(at):
        total = qsum[level, :, at:at + HD].astype(F32)
        for d in range(1, deep):
            total = total + qz[d - 1, :, at:at + HD].astype(F32)
        return (total * factor[:, :1]).astype(BF)

    for h in range(tile // HD):
        queries = head_part(h * HD)
        keys = head_part(tile + h * HD)
        values = head_part(2 * tile + h * HD)
        scores = lax.dot_general(
            queries, keys, (((1,), (1,)), ((), ())), preferred_element_type=F32
        ) * HD ** (-0.5)
        scores = jnp.where(allowed, scores, -1e30)
        weights = jnp.exp(scores - jnp.max(scores, axis=1, keepdims=True))
        weights = (weights / jnp.sum(weights, axis=1, keepdims=True)).astype(BF)
        mixall[row, :, h * HD:(h + 1) * HD] = mm(weights, values).astype(BF)
    copies = [
        send(mixall.at[row], mixall.at[row], mz_s.at[d], mz_r.at[d], (level_at(d) * 2 + core, col))
        for d in range(1, deep)
    ]
    sibs = [send(mixall.at[row], mixall.at[row], ms_s.at[0], ms_r.at[0], sibling)]
    for d in range(1, deep):
        copies[d - 1].wait_recv()
        source = level_at(deep - d) * 2 + core
        sibs.append(send(mixall.at[source], mixall.at[source], ms_s.at[d], ms_r.at[d], sibling))
    for copy in sibs:
        copy.wait_recv()

    for i in range(n_qkv, n_out):
        fetch(i).wait()

    @pl.loop(0, width // tile)
    def _(n):
        across = pl.ds(pl.multiple_of(n * tile, tile), tile)
        total = jnp.zeros((tokens, tile), F32)
        for r in range(rows):
            i = n_qkv + r * tile // width
            down = r * tile % width
            total = total + mm(mixall[r], ring[i % SLOTS, down:down + tile, across])
        part[1, :, across] = total.astype(BF)

    fetch_after(n_qkv, n_out)
    total = reduce_cols(1)
    sq_copies = spread_norm(1, (resid[...].astype(F32) + total).astype(BF), gain_f)

    def rows_of(level_of):
        return pl.ds(pl.multiple_of(level_of * mine, mine), mine)

    def half_of(core_of):
        return pl.ds(pl.multiple_of(core_of * half, half), half)

    def product(c):
        for k in range(2):
            i = n_out + 2 * c + k
            fetch(i).wait()

            @pl.loop(0, width // tile)
            def _(n):
                across = pl.ds(pl.multiple_of(n * tile, tile), tile)
                to = pl.ds(pl.multiple_of(k * width + n * tile, tile), tile)
                gp[c, :, to] = mm(scaled[...], ring[i % SLOTS, :, across]).astype(BF)

        fetch_after(n_out + 2 * c, n_out + 2 * c + 2)
        return send(gp.at[c, half_of(other), :], gsib.at[c], gs_s.at[c], gs_r.at[c], sibling)

    def presum(c, copy):
        copy.wait_recv()
        gsum[c] = (gp[c, half_of(core), :].astype(F32) + gsib[c].astype(F32)).astype(BF)
        return [
            send(
                gsum.at[c, rows_of(level_at(d)), :], gz.at[c, d - 1],
                gz_s.at[c, d], gz_r.at[c, d], (level_at(d) * 2 + core, col),
            )
            for d in range(1, deep)
        ]

    own_at = pl.multiple_of(core * half + level * mine, mine)

    def activate(c, copies):
        for copy in copies:
            copy.wait_recv()
        total = gsum[c, rows_of(level), :].astype(F32)
        for d in range(1, deep):
            total = total + gz[c, d - 1].astype(F32)
        total = total * factor[pl.ds(own_at, mine), :1]
        gate, up = total[:, :width], total[:, width:]
        act[c, pl.ds(own_at, mine), :] = (gate * (1.0 / (1.0 + jnp.exp(-gate))) * up).astype(BF)
        return [
            send(
                act.at[c, pl.ds(own_at, mine), :], act.at[c, pl.ds(own_at, mine), :],
                az_s.at[c, d], az_r.at[c, d], (level_at(d) * 2 + core, col),
            )
            for d in range(1, deep)
        ]

    def forward(c, copies):
        for copy in copies:
            copy.wait_recv()
        return send(act.at[c, half_of(core), :], act.at[c, half_of(core), :], as_s.at[c], as_r.at[c], sibling)

    def down(c, copy):
        copy.wait_recv()
        i = n_up + c
        fetch(i).wait()

        @pl.loop(0, width // tile)
        def _(n):
            across = pl.ds(pl.multiple_of(n * tile, tile), tile)
            term = mm(act[c], ring[i % SLOTS, :, across])
            if c:
                term = term + dacc[:, across]
            if c < chunks - 1:
                dacc[:, across] = term
            else:
                part[2, :, across] = term.astype(BF)

    first, second, third, fourth = {}, {}, {}, {}
    for c in range(chunks + 1):
        if c < chunks:
            first[c] = product(c)
        if c:
            second[c - 1] = presum(c - 1, first[c - 1])
    take_factor(1, sq_copies)
    for c in range(chunks + 2):
        if c < chunks:
            third[c] = activate(c, second[c])
        if 1 <= c <= chunks:
            fourth[c - 1] = forward(c - 1, third[c - 1])
        if c >= 2:
            down(c - 2, fourth[c - 2])

    total = reduce_cols(2)
    final = (resid[...].astype(F32) + total).astype(BF)

    strip = width // quarter
    for q in range(quarter):
        pick = one_hot(
            (rows * SUB, share),
            lambda i, m: (i // SUB == m // here) & (i % here == m % here) & ((i % SUB) // here == q),
        )
        term = mm(pick, final[:, q * strip:(q + 1) * strip])
        if q == 0:
            total = term
        else:
            total = total + term
    fsend[...] = total.astype(BF)
    me_at = pl.multiple_of(row * SUB, SUB)
    frecv[pl.ds(me_at, SUB), :] = fsend[pl.ds(me_at, SUB), :]
    copies = []
    for d in range(1, rows):
        copies.append(send(
            fsend.at[pl.ds(pl.multiple_of(row_at(d) * SUB, SUB), SUB), :], frecv.at[pl.ds(me_at, SUB), :],
            fin_s.at[d], fin_r.at[d], (row_at(d), col),
        ))
    for copy in copies:
        copy.wait_recv()
    for q in range(quarter):
        pick = one_hot(
            (here * cols, SUB), lambda i, m: (m % here == i // cols) & (m // here == q)
        )
        for s in range(rows):
            to = slice(s * width + q * strip, s * width + (q + 1) * strip)
            out[:, to] = (chars[:, to].astype(F32) + mm(pick, frecv[s * SUB:(s + 1) * SUB, :])).astype(BF)
    for copy in pending:
        copy.wait_send()


def fused_layer(chars, pool_w, gain_a, wq, wk, wv, wo, gain_f, wg, wu, wd):
    rows = lax.axis_size("row")
    cols = lax.axis_size("col")
    width = pool_w.shape[1]
    here = chars.shape[0] // POOL
    tokens = here * rows * cols
    chunks = wg.shape[1] // width
    deep = rows // 2
    share, mine, half = tokens // cols, tokens // rows, tokens // 2
    tile = wq.shape[1] // rows
    piece = chars.shape[1] * here // SUB
    dma = pltpu.SemaphoreType.DMA
    scratch = [
        pltpu.VMEM((SLOTS, width, width), BF), dma((64,)),
        pltpu.VMEM((cols * SUB, piece), BF), pltpu.VMEM((cols * SUB, piece), BF),
        pltpu.VMEM((tokens, chars.shape[1]), BF),
        pltpu.VMEM((3, tokens, width), BF), pltpu.VMEM((3, cols - 1, share, width), BF),
        pltpu.VMEM((2, tokens, width), BF), pltpu.VMEM((tokens, width), BF), pltpu.VMEM((share, width), BF),
        pltpu.VMEM((2, 8, tokens), F32), pltpu.VMEM((2, rows - 1, 8, tokens), F32), pltpu.VMEM((tokens, tokens), F32),
        pltpu.VMEM((2, deep, tokens, 3 * tile), BF), pltpu.VMEM((deep, tokens, 3 * tile), BF),
        pltpu.VMEM((deep, tokens, 3 * tile), BF), pltpu.VMEM((deep - 1, tokens, 3 * tile), BF),
        pltpu.VMEM((rows, tokens, tile), BF),
        pltpu.VMEM((chunks, tokens, 2 * width), BF), pltpu.VMEM((chunks, half, 2 * width), BF),
        pltpu.VMEM((chunks, half, 2 * width), BF), pltpu.VMEM((chunks, deep - 1, mine, 2 * width), BF),
        pltpu.VMEM((chunks, tokens, width), BF), pltpu.VMEM((tokens, width), F32),
        pltpu.VMEM((rows * SUB, width * here // SUB), BF), pltpu.VMEM((rows * SUB, width * here // SUB), BF),
        dma((cols,)), dma((cols,)), dma((deep,)), dma((deep,)), dma((deep,)), dma((deep,)),
        dma((3, cols)), dma((3, cols)), dma((2, cols)), dma((2, cols)), dma((2, rows)), dma((2, rows)),
        dma, dma, dma((deep,)), dma((deep,)), dma((deep,)), dma((deep,)), dma((deep,)), dma((deep,)),
        dma((chunks,)), dma((chunks,)), dma((chunks, deep)), dma((chunks, deep)),
        dma((chunks, deep)), dma((chunks, deep)), dma((chunks,)), dma((chunks,)), dma((rows,)), dma((rows,)),
    ]
    vmem, hbm = pl.BlockSpec(memory_space=pltpu.VMEM), pl.BlockSpec(memory_space=pl.ANY)
    return pl.pallas_call(
        functools.partial(layer_kernel, (rows, cols, tokens, width, here, chunks)),
        out_shape=jax.ShapeDtypeStruct(chars.shape, chars.dtype),
        in_specs=[vmem, hbm, vmem, hbm, hbm, hbm, hbm, vmem, hbm, hbm, hbm],
        out_specs=vmem,
        scratch_shapes=scratch,
        compiler_params=pltpu.CompilerParams(
            collective_id=0, has_side_effects=True, vmem_limit_bytes=63 * 1024 * 1024
        ),
    )(chars, pool_w, gain_a.reshape(1, -1), wq, wk, wv, wo, gain_f.reshape(1, -1), wg, wu, wd)


def fits(chars, pool_w, wq, wg):
    rows, cols = lax.axis_size("row"), lax.axis_size("col")
    width = pool_w.shape[1]
    here = chars.shape[0] // POOL
    tokens = here * rows * cols
    return (
        cols == POOL and rows % 2 == 0 and tokens == HD and SUB % here == 0
        and (wq.shape[1] // HD) % rows == 0 and tokens // rows == SUB
        and wq.shape[1] % width == 0 and wg.shape[1] % width == 0
        and width % (wq.shape[1] // rows) == 0
    )


def on_device(
    chars, pool_weight, gain_attn, w_query, w_key, w_value, w_out, gain_ffn, w_gate, w_up, w_down
):
    args = (chars, pool_weight, gain_attn, w_query, w_key, w_value, w_out, gain_ffn, w_gate, w_up, w_down)
    if fits(chars, pool_weight, w_query, w_gate):
        return fused_layer(*args)
    return by_collectives(*args)


def solution(mesh):
    return jax.shard_map(
        on_device,
        mesh=mesh,
        in_specs=(
            P(("row", "col"), None),
            P("col", "row"),
            P("row"),
            P("row", "col"),
            P("row", "col"),
            P("row", "col"),
            P("col", "row"),
            P("row"),
            P("row", "col"),
            P("row", "col"),
            P("col", "row"),
        ),
        out_specs=P(("row", "col"), None),
        check_vma=False,
    )
```

```python
import functools

import jax
import jax.numpy as jnp
from jax import lax
from jax.experimental import pallas as pl
from jax.experimental.pallas import tpu as pltpu
from jax.sharding import PartitionSpec as P

D = 8192
HD = 128
POOL = 4


EPS = 1e-05


def square_sum(hidden):
    values = hidden.astype(jnp.float32)
    return jnp.sum(values * values, axis=-1)


def norm_apply(hidden, totals, gain):
    factor = lax.rsqrt(totals / D + EPS)[..., None]
    return (hidden.astype(jnp.float32) * factor * gain.astype(jnp.float32)).astype(jnp.bfloat16)


def attend(queries, keys_part, values_part, offset):
    query_count = queries.shape[0]
    key_count = keys_part.shape[0]
    query_heads = queries.reshape(query_count, -1, HD)
    key_heads = keys_part.reshape(key_count, -1, HD)
    value_heads = values_part.reshape(key_count, -1, HD)
    scores = jnp.einsum(
        "qhd,khd->hqk", query_heads, key_heads, preferred_element_type=jnp.float32
    ) * HD ** (-0.5)
    query_places = offset + jnp.arange(query_count, dtype=jnp.int32)
    key_places = jnp.arange(key_count, dtype=jnp.int32)
    allowed = query_places[:, None] >= key_places[None, :]
    scores = jnp.where(allowed[None], scores, jnp.float32(-1e30))
    highest = jnp.max(scores, axis=-1, keepdims=True)
    weights = jnp.exp(scores - highest)
    weights = (weights / jnp.sum(weights, axis=-1, keepdims=True)).astype(jnp.bfloat16)
    mixed = jnp.einsum("hqk,khd->qhd", weights, value_heads, preferred_element_type=jnp.float32)
    return mixed.astype(jnp.bfloat16).reshape(query_count, -1)


def by_collectives(
    chars, pool_weight, gain_attn, w_query, w_key, w_value, w_out, gain_ffn, w_gate, w_up, w_down
):
    rows_count = lax.axis_size("row")
    cols_count = lax.axis_size("col")
    char_rows = chars.shape[0]
    tokens_here = char_rows // POOL
    feature_block = pool_weight.shape[1]
    grouped = chars.reshape(1, 1, tokens_here, POOL * chars.shape[1])
    spread = lax.all_to_all(grouped, "col", split_axis=3, concat_axis=1, tiled=True)
    piece = lax.all_gather(spread, "row", axis=0, tiled=True)
    pool_terms = jnp.dot(
        piece.reshape(-1, piece.shape[3]), pool_weight, preferred_element_type=jnp.float32
    )
    pool_terms = pool_terms.reshape(rows_count, cols_count, tokens_here, feature_block)
    pooled = lax.psum_scatter(
        pool_terms.astype(jnp.bfloat16), "col", scatter_dimension=1, tiled=True
    )
    attn_totals = lax.psum(square_sum(pooled), "row")
    normed_attn = norm_apply(pooled, attn_totals, gain_attn)
    gathered = lax.all_gather(normed_attn, "col", axis=1, tiled=True).reshape(-1, feature_block)
    seq_length = gathered.shape[0]
    block_rows = seq_length // rows_count
    slab = gathered
    queries = lax.psum_scatter(
        jnp.dot(slab, w_query, preferred_element_type=jnp.float32).astype(jnp.bfloat16),
        "row",
        scatter_dimension=0,
        tiled=True,
    )
    slab = gathered
    pair_local = lax.psum_scatter(
        jnp.concatenate(
            [
                jnp.dot(slab, w_key, preferred_element_type=jnp.float32),
                jnp.dot(slab, w_value, preferred_element_type=jnp.float32),
            ],
            axis=1,
        ).astype(jnp.bfloat16),
        "row",
        scatter_dimension=0,
        tiled=True,
    )
    pair_whole = lax.all_gather(pair_local, "row", axis=0, tiled=True)
    head_columns = w_query.shape[1]
    keys_part = pair_whole[:, :head_columns]
    values_part = pair_whole[:, head_columns:]
    mixed = attend(queries, keys_part, values_part, lax.axis_index("row") * block_rows)
    out_terms = jnp.dot(
        lax.all_gather(mixed, "row", axis=0, tiled=True), w_out, preferred_element_type=jnp.float32
    )
    out_terms = out_terms.reshape(rows_count, cols_count, tokens_here, feature_block)
    attn_total = lax.psum_scatter(
        out_terms.astype(jnp.bfloat16), "col", scatter_dimension=1, tiled=True
    ).astype(jnp.float32)
    first = (pooled.astype(jnp.float32) + attn_total).astype(jnp.bfloat16)
    ffn_totals = lax.psum(square_sum(first), "row")
    normed_ffn = norm_apply(first, ffn_totals, gain_ffn)
    gathered_ffn = lax.all_gather(normed_ffn, "col", axis=1, tiled=True).reshape(-1, feature_block)
    hidden_local = w_gate.shape[1]
    slab = gathered_ffn
    hidden_pair = lax.psum_scatter(
        jnp.concatenate(
            [
                jnp.dot(slab, w_gate, preferred_element_type=jnp.float32),
                jnp.dot(slab, w_up, preferred_element_type=jnp.float32),
            ],
            axis=1,
        ).astype(jnp.bfloat16),
        "row",
        scatter_dimension=0,
        tiled=True,
    ).astype(jnp.float32)
    activated = (jax.nn.silu(hidden_pair[:, :hidden_local]) * hidden_pair[:, hidden_local:]).astype(
        jnp.bfloat16
    )
    down_terms = jnp.dot(
        lax.all_gather(activated, "row", axis=0, tiled=True),
        w_down,
        preferred_element_type=jnp.float32,
    )
    down_terms = down_terms.reshape(rows_count, cols_count, tokens_here, feature_block)
    ffn_total = lax.psum_scatter(
        down_terms.astype(jnp.bfloat16), "col", scatter_dimension=1, tiled=True
    ).astype(jnp.float32)
    second = (first.astype(jnp.float32) + ffn_total).astype(jnp.bfloat16)
    returned = lax.all_to_all(second, "row", split_axis=0, concat_axis=3, tiled=True)
    expanded = jnp.repeat(returned.reshape(tokens_here, -1), POOL, axis=0)
    return (chars.astype(jnp.float32) + expanded.astype(jnp.float32)).astype(jnp.bfloat16)


MESH = pl.DeviceIdType.MESH
BF = jnp.bfloat16
F32 = jnp.float32
SLOTS = 20
SUB = 16


def one_hot(shape, test):
    rows_at = lax.broadcasted_iota(jnp.int32, shape, 0)
    cols_at = lax.broadcasted_iota(jnp.int32, shape, 1)
    return jnp.where(test(rows_at, cols_at), 1.0, 0.0).astype(BF)


def mm(left, right):
    return jnp.dot(left, right, preferred_element_type=F32)


def layer_kernel(
    sizes, chars, pool_w, gain_a, wq, wk, wv, wo, gain_f, wg, wu, wd, out,
    ring, ring_sem,
    stage, xin, xall, part, crecv, hall, scaled, resid,
    sq, sqrecv, factor,
    qp, qsib, qsum, qz, mixall,
    gp, gsib, gsum, gz, act, dacc,
    fsend, frecv,
    a2a_s, a2a_r, xz_s, xz_r, xs_s, xs_r, rs_s, rs_r, ag_s, ag_r, sq_s, sq_r,
    qs_s, qs_r, qz_s, qz_r, mz_s, mz_r, ms_s, ms_r,
    gs_s, gs_r, gz_s, gz_r, az_s, az_r, as_s, as_r, fin_s, fin_r,
):
    rows, cols, tokens, width, here, chunks = sizes
    deep = rows // 2
    quarter = SUB // here
    piece = chars.shape[1] // quarter
    share = tokens // cols
    mine = tokens // rows
    half = tokens // 2
    head_cols = wq.shape[1] // rows
    tile = head_cols
    row = lax.axis_index("row")
    col = lax.axis_index("col")
    level = lax.div(row, 2)
    core = lax.rem(row, 2)
    other = 1 - core
    sibling = (level * 2 + other, col)
    pending = []

    def send(source, target, s_sem, r_sem, where):
        copy = pltpu.make_async_remote_copy(
            src_ref=source, dst_ref=target, send_sem=s_sem, recv_sem=r_sem,
            device_id=where, device_id_type=MESH,
        )
        copy.start()
        pending.append(copy)
        return copy

    def col_at(d):
        return lax.rem(col + d, cols)

    def level_at(d):
        return lax.rem(level + d, deep)

    def row_at(d):
        return lax.rem(row + d, rows)

    blocks = [(pool_w, i, 0) for i in range(pool_w.shape[0] // width)]
    n_pool = len(blocks)
    for weight in (wq, wk, wv):
        blocks += [(weight, 0, i) for i in range(weight.shape[1] // width)]
    n_qkv = len(blocks)
    blocks += [(wo, i, 0) for i in range(wo.shape[0] // width)]
    n_out = len(blocks)
    for i in range(chunks):
        blocks += [(wg, 0, i), (wu, 0, i)]
    n_up = len(blocks)
    blocks += [(wd, i, 0) for i in range(chunks)]

    def fetch(i):
        ref, down, across = blocks[i]
        return pltpu.make_async_copy(
            ref.at[pl.ds(down * width, width), pl.ds(across * width, width)],
            ring.at[i % SLOTS], ring_sem.at[i],
        )

    def fetch_after(first, last):
        for i in range(first, last):
            if i + SLOTS < len(blocks):
                fetch(i + SLOTS).start()

    for i in range(min(SLOTS, len(blocks))):
        fetch(i).start()

    barrier = pltpu.get_barrier_semaphore()
    for d in range(1, cols):
        pl.semaphore_signal(barrier, inc=1, device_id=(row, col_at(d)), device_id_type=MESH)
    for d in range(1, rows):
        pl.semaphore_signal(barrier, inc=1, device_id=(row_at(d), col), device_id_type=MESH)

    for q in range(quarter):
        pick = one_hot(
            (cols * SUB, here * cols),
            lambda i, m: (m == (i % here) * cols + i // SUB) & ((i % SUB) // here == q),
        )
        term = mm(pick, chars[:, q * piece:(q + 1) * piece])
        if q == 0:
            total = term
        else:
            total = total + term
    stage[...] = total.astype(BF)
    at = pl.multiple_of(col * SUB, SUB)
    xin[pl.ds(at, SUB), :] = stage[pl.ds(at, SUB), :]
    pl.semaphore_wait(barrier, cols + rows - 2)
    copies = []
    for d in range(1, cols):
        copies.append(send(
            stage.at[pl.ds(pl.multiple_of(col_at(d) * SUB, SUB), SUB), :], xin.at[pl.ds(at, SUB), :],
            a2a_s.at[d], a2a_r.at[d], (row, col_at(d)),
        ))
    for copy in copies:
        copy.wait_recv()
    here_at = pl.multiple_of(row * mine, mine)

    def x_rows(level_of, core_of, q):
        at = pl.multiple_of((level_of * 2 + core_of) * mine, mine)
        return xall.at[pl.ds(at, mine), q * piece:(q + 1) * piece]

    across_z, sibs = {}, {}
    for q in range(quarter):
        pick = one_hot(
            (mine, cols * SUB),
            lambda i, m: (m // SUB == i // here) & (m % here == i % here) & ((m % SUB) // here == q),
        )
        xall[pl.ds(here_at, mine), q * piece:(q + 1) * piece] = mm(pick, xin[...]).astype(BF)
        mine_q = x_rows(level, core, q)
        for d in range(1, deep):
            across_z[q, d] = send(
                mine_q, mine_q, xz_s.at[q, d], xz_r.at[q, d], (level_at(d) * 2 + core, col)
            )
        sibs[q] = [send(mine_q, mine_q, xs_s.at[q, 0], xs_r.at[q, 0], sibling)]

    def forward_piece(q):
        for d in range(1, deep):
            across_z[q, d].wait_recv()
            came = x_rows(level_at(deep - d), core, q)
            sibs[q].append(send(came, came, xs_s.at[q, d], xs_r.at[q, d], sibling))

    def pool_piece(q):
        for copy in sibs[q]:
            copy.wait_recv()
        ids = range(q * n_pool // quarter, (q + 1) * n_pool // quarter)
        for i in ids:
            fetch(i).wait()

        @pl.loop(0, width // tile)
        def _(n):
            across = pl.ds(pl.multiple_of(n * tile, tile), tile)
            if q:
                total = dacc[:, across]
            else:
                total = jnp.zeros((tokens, tile), F32)
            for i in ids:
                total = total + mm(xall[:, i * width:(i + 1) * width], ring[i % SLOTS, :, across])
            if q < quarter - 1:
                dacc[:, across] = total
            else:
                part[0, :, across] = mm(order, total.astype(BF)).astype(BF)

    order = one_hot(
        (tokens, tokens),
        lambda i, m: m == ((i % share) // here) * mine + (i // share) * here + i % here,
    )
    for q in range(quarter + 1):
        if q < quarter:
            forward_piece(q)
        if q:
            pool_piece(q - 1)
    fetch_after(0, n_pool)
    share_at = pl.multiple_of(col * share, share)
    my_share = pl.ds(share_at, share)

    def reduce_cols(step):
        copies = []
        for d in range(1, cols):
            copies.append(send(
                part.at[step, pl.ds(pl.multiple_of(col_at(d) * share, share), share), :],
                crecv.at[step, d - 1], rs_s.at[step, d], rs_r.at[step, d], (row, col_at(d)),
            ))
        for copy in copies:
            copy.wait_recv()
        total = part[step, my_share, :].astype(F32)
        for d in range(1, cols):
            total = total + crecv[step, d - 1].astype(F32)
        return total

    def spread_norm(step, values, gain):
        resid[...] = values
        hall[step, my_share, :] = values
        copies = []
        for d in range(1, cols):
            copies.append(send(
                hall.at[step, my_share, :], hall.at[step, my_share, :],
                ag_s.at[step, d], ag_r.at[step, d], (row, col_at(d)),
            ))
        for copy in copies:
            copy.wait_recv()
        whole = hall[step].astype(F32)
        scaled[...] = (whole * gain[...].astype(F32)).astype(BF)
        squares = jnp.sum(whole * whole, axis=1, keepdims=True)
        flat = jnp.broadcast_to(squares, (tokens, tokens)).T
        sq[step] = flat[:8]
        return [
            send(sq.at[step], sqrecv.at[step, d - 1], sq_s.at[step, d], sq_r.at[step, d], (row_at(d), col))
            for d in range(1, rows)
        ]

    def take_factor(step, copies):
        for copy in copies:
            copy.wait_recv()
        total = sq[step]
        for d in range(1, rows):
            total = total + sqrecv[step, d - 1]
        line = lax.rsqrt(total / (rows * width) + EPS)
        factor[...] = jnp.broadcast_to(line[:1], (tokens, tokens)).T

    sq_copies = spread_norm(0, reduce_cols(0).astype(BF), gain_a)

    per = width // tile
    per_kind = wq.shape[1] // width
    copies, swaps = [], {}

    def qkv_product(kind):
        for b in range(per_kind):
            i = n_pool + kind * per_kind + b
            fetch(i).wait()

            @pl.loop(0, per)
            def _(n):
                owner = b * per + n
                across = pl.ds(pl.multiple_of(n * tile, tile), tile)
                qp[kind, lax.rem(owner, 2), lax.div(owner, 2)] = mm(
                    scaled[...], ring[i % SLOTS, :, across]
                ).astype(BF)

        fetch_after(n_pool + kind * per_kind, n_pool + (kind + 1) * per_kind)
        swaps[kind] = send(qp.at[kind, other], qsib.at[kind], qs_s.at[kind], qs_r.at[kind], sibling)

    def qkv_presum(kind):
        swaps[kind].wait_recv()
        for d in list(range(1, deep)) + [0]:
            there = level_at(d)
            qsum[kind, there] = (qp[kind, core, there].astype(F32) + qsib[kind, there].astype(F32)).astype(BF)
            if d:
                copies.append(send(
                    qsum.at[kind, there], qz.at[kind, d - 1],
                    qz_s.at[kind, d], qz_r.at[kind, d], (there * 2 + core, col),
                ))

    for kind in range(4):
        if kind < 3:
            qkv_product(kind)
        if kind:
            qkv_presum(kind - 1)
    take_factor(0, sq_copies)
    for copy in copies:
        copy.wait_recv()
    places_i = lax.broadcasted_iota(jnp.int32, (tokens, tokens), 0)
    places_j = lax.broadcasted_iota(jnp.int32, (tokens, tokens), 1)

    def true_place(i):
        return ((i % share) // here) * mine + (i // share) * here + i % here

    allowed = true_place(places_i) >= true_place(places_j)

    def head_part(kind, at):
        total = qsum[kind, level, :, at:at + HD].astype(F32)
        for d in range(1, deep):
            total = total + qz[kind, d - 1, :, at:at + HD].astype(F32)
        return (total * factor[:, :1]).astype(BF)

    for h in range(tile // HD):
        queries = head_part(0, h * HD)
        keys = head_part(1, h * HD)
        values = head_part(2, h * HD)
        scores = lax.dot_general(
            queries, keys, (((1,), (1,)), ((), ())), preferred_element_type=F32
        ) * HD ** (-0.5)
        scores = jnp.where(allowed, scores, -1e30)
        weights = jnp.exp(scores - jnp.max(scores, axis=1, keepdims=True))
        weights = (weights / jnp.sum(weights, axis=1, keepdims=True)).astype(BF)
        mixall[row, :, h * HD:(h + 1) * HD] = mm(weights, values).astype(BF)
    copies = [
        send(mixall.at[row], mixall.at[row], mz_s.at[d], mz_r.at[d], (level_at(d) * 2 + core, col))
        for d in range(1, deep)
    ]
    sibs = [send(mixall.at[row], mixall.at[row], ms_s.at[0], ms_r.at[0], sibling)]
    for d in range(1, deep):
        copies[d - 1].wait_recv()
        source = level_at(deep - d) * 2 + core
        sibs.append(send(mixall.at[source], mixall.at[source], ms_s.at[d], ms_r.at[d], sibling))
    for copy in sibs:
        copy.wait_recv()

    for i in range(n_qkv, n_out):
        fetch(i).wait()

    @pl.loop(0, width // tile)
    def _(n):
        across = pl.ds(pl.multiple_of(n * tile, tile), tile)
        total = jnp.zeros((tokens, tile), F32)
        for r in range(rows):
            i = n_qkv + r * tile // width
            down = r * tile % width
            total = total + mm(mixall[r], ring[i % SLOTS, down:down + tile, across])
        part[1, :, across] = total.astype(BF)

    fetch_after(n_qkv, n_out)
    total = reduce_cols(1)
    sq_copies = spread_norm(1, (resid[...].astype(F32) + total).astype(BF), gain_f)

    def rows_of(level_of):
        return pl.ds(pl.multiple_of(level_of * mine, mine), mine)

    def half_of(core_of):
        return pl.ds(pl.multiple_of(core_of * half, half), half)

    def product(c):
        for k in range(2):
            i = n_out + 2 * c + k
            fetch(i).wait()

            @pl.loop(0, width // tile)
            def _(n):
                across = pl.ds(pl.multiple_of(n * tile, tile), tile)
                to = pl.ds(pl.multiple_of(k * width + n * tile, tile), tile)
                gp[c, :, to] = mm(scaled[...], ring[i % SLOTS, :, across]).astype(BF)

        fetch_after(n_out + 2 * c, n_out + 2 * c + 2)
        return send(gp.at[c, half_of(other), :], gsib.at[c], gs_s.at[c], gs_r.at[c], sibling)

    def presum(c, copy):
        copy.wait_recv()
        gsum[c] = (gp[c, half_of(core), :].astype(F32) + gsib[c].astype(F32)).astype(BF)
        return [
            send(
                gsum.at[c, rows_of(level_at(d)), :], gz.at[c, d - 1],
                gz_s.at[c, d], gz_r.at[c, d], (level_at(d) * 2 + core, col),
            )
            for d in range(1, deep)
        ]

    own_at = pl.multiple_of(core * half + level * mine, mine)

    def activate(c, copies):
        for copy in copies:
            copy.wait_recv()
        total = gsum[c, rows_of(level), :].astype(F32)
        for d in range(1, deep):
            total = total + gz[c, d - 1].astype(F32)
        total = total * factor[pl.ds(own_at, mine), :1]
        gate, up = total[:, :width], total[:, width:]
        act[c, pl.ds(own_at, mine), :] = (gate * (1.0 / (1.0 + jnp.exp(-gate))) * up).astype(BF)
        return [
            send(
                act.at[c, pl.ds(own_at, mine), :], act.at[c, pl.ds(own_at, mine), :],
                az_s.at[c, d], az_r.at[c, d], (level_at(d) * 2 + core, col),
            )
            for d in range(1, deep)
        ]

    def forward(c, copies):
        for copy in copies:
            copy.wait_recv()
        return send(act.at[c, half_of(core), :], act.at[c, half_of(core), :], as_s.at[c], as_r.at[c], sibling)

    def down(c, copy):
        copy.wait_recv()
        i = n_up + c
        fetch(i).wait()

        @pl.loop(0, width // tile)
        def _(n):
            across = pl.ds(pl.multiple_of(n * tile, tile), tile)
            term = mm(act[c], ring[i % SLOTS, :, across])
            if c:
                term = term + dacc[:, across]
            if c < chunks - 1:
                dacc[:, across] = term
            else:
                part[2, :, across] = term.astype(BF)

    first, second, third, fourth = {}, {}, {}, {}
    for c in range(chunks + 1):
        if c < chunks:
            first[c] = product(c)
        if c:
            second[c - 1] = presum(c - 1, first[c - 1])
    take_factor(1, sq_copies)
    for c in range(chunks + 2):
        if c < chunks:
            third[c] = activate(c, second[c])
        if 1 <= c <= chunks:
            fourth[c - 1] = forward(c - 1, third[c - 1])
        if c >= 2:
            down(c - 2, fourth[c - 2])

    total = reduce_cols(2)
    final = (resid[...].astype(F32) + total).astype(BF)

    strip = width // quarter
    for q in range(quarter):
        pick = one_hot(
            (rows * SUB, share),
            lambda i, m: (i // SUB == m // here) & (i % here == m % here) & ((i % SUB) // here == q),
        )
        term = mm(pick, final[:, q * strip:(q + 1) * strip])
        if q == 0:
            total = term
        else:
            total = total + term
    fsend[...] = total.astype(BF)
    me_at = pl.multiple_of(row * SUB, SUB)
    frecv[pl.ds(me_at, SUB), :] = fsend[pl.ds(me_at, SUB), :]
    copies = []
    for d in range(1, rows):
        copies.append(send(
            fsend.at[pl.ds(pl.multiple_of(row_at(d) * SUB, SUB), SUB), :], frecv.at[pl.ds(me_at, SUB), :],
            fin_s.at[d], fin_r.at[d], (row_at(d), col),
        ))
    for copy in copies:
        copy.wait_recv()
    for q in range(quarter):
        pick = one_hot(
            (here * cols, SUB), lambda i, m: (m % here == i // cols) & (m // here == q)
        )
        for s in range(rows):
            to = slice(s * width + q * strip, s * width + (q + 1) * strip)
            out[:, to] = (chars[:, to].astype(F32) + mm(pick, frecv[s * SUB:(s + 1) * SUB, :])).astype(BF)
    for copy in pending:
        copy.wait_send()


def fused_layer(chars, pool_w, gain_a, wq, wk, wv, wo, gain_f, wg, wu, wd):
    rows = lax.axis_size("row")
    cols = lax.axis_size("col")
    width = pool_w.shape[1]
    here = chars.shape[0] // POOL
    tokens = here * rows * cols
    chunks = wg.shape[1] // width
    deep = rows // 2
    share, mine, half = tokens // cols, tokens // rows, tokens // 2
    tile = wq.shape[1] // rows
    piece = chars.shape[1] * here // SUB
    dma = pltpu.SemaphoreType.DMA
    scratch = [
        pltpu.VMEM((SLOTS, width, width), BF), dma((64,)),
        pltpu.VMEM((cols * SUB, piece), BF), pltpu.VMEM((cols * SUB, piece), BF),
        pltpu.VMEM((tokens, chars.shape[1]), BF),
        pltpu.VMEM((3, tokens, width), BF), pltpu.VMEM((3, cols - 1, share, width), BF),
        pltpu.VMEM((2, tokens, width), BF), pltpu.VMEM((tokens, width), BF), pltpu.VMEM((share, width), BF),
        pltpu.VMEM((2, 8, tokens), F32), pltpu.VMEM((2, rows - 1, 8, tokens), F32), pltpu.VMEM((tokens, tokens), F32),
        pltpu.VMEM((3, 2, deep, tokens, tile), BF), pltpu.VMEM((3, deep, tokens, tile), BF),
        pltpu.VMEM((3, deep, tokens, tile), BF), pltpu.VMEM((3, deep - 1, tokens, tile), BF),
        pltpu.VMEM((rows, tokens, tile), BF),
        pltpu.VMEM((chunks, tokens, 2 * width), BF), pltpu.VMEM((chunks, half, 2 * width), BF),
        pltpu.VMEM((chunks, half, 2 * width), BF), pltpu.VMEM((chunks, deep - 1, mine, 2 * width), BF),
        pltpu.VMEM((chunks, tokens, width), BF), pltpu.VMEM((tokens, width), F32),
        pltpu.VMEM((rows * SUB, width * here // SUB), BF), pltpu.VMEM((rows * SUB, width * here // SUB), BF),
        dma((cols,)), dma((cols,)), dma((SUB // here, deep)), dma((SUB // here, deep)), dma((SUB // here, deep)), dma((SUB // here, deep)),
        dma((3, cols)), dma((3, cols)), dma((2, cols)), dma((2, cols)), dma((2, rows)), dma((2, rows)),
        dma((3,)), dma((3,)), dma((3, deep)), dma((3, deep)), dma((deep,)), dma((deep,)), dma((deep,)), dma((deep,)),
        dma((chunks,)), dma((chunks,)), dma((chunks, deep)), dma((chunks, deep)),
        dma((chunks, deep)), dma((chunks, deep)), dma((chunks,)), dma((chunks,)), dma((rows,)), dma((rows,)),
    ]
    vmem, hbm = pl.BlockSpec(memory_space=pltpu.VMEM), pl.BlockSpec(memory_space=pl.ANY)
    return pl.pallas_call(
        functools.partial(layer_kernel, (rows, cols, tokens, width, here, chunks)),
        out_shape=jax.ShapeDtypeStruct(chars.shape, chars.dtype),
        in_specs=[vmem, hbm, vmem, hbm, hbm, hbm, hbm, vmem, hbm, hbm, hbm],
        out_specs=vmem,
        scratch_shapes=scratch,
        compiler_params=pltpu.CompilerParams(
            collective_id=0, has_side_effects=True, vmem_limit_bytes=63 * 1024 * 1024
        ),
    )(chars, pool_w, gain_a.reshape(1, -1), wq, wk, wv, wo, gain_f.reshape(1, -1), wg, wu, wd)


def fits(chars, pool_w, wq, wg):
    rows, cols = lax.axis_size("row"), lax.axis_size("col")
    width = pool_w.shape[1]
    here = chars.shape[0] // POOL
    tokens = here * rows * cols
    return (
        cols == POOL and rows % 2 == 0 and tokens == HD and SUB % here == 0
        and (wq.shape[1] // HD) % rows == 0 and tokens // rows == SUB
        and wq.shape[1] % width == 0 and wg.shape[1] % width == 0
        and width % (wq.shape[1] // rows) == 0
    )


def on_device(
    chars, pool_weight, gain_attn, w_query, w_key, w_value, w_out, gain_ffn, w_gate, w_up, w_down
):
    args = (chars, pool_weight, gain_attn, w_query, w_key, w_value, w_out, gain_ffn, w_gate, w_up, w_down)
    if fits(chars, pool_weight, w_query, w_gate):
        return fused_layer(*args)
    return by_collectives(*args)


def solution(mesh):
    return jax.shard_map(
        on_device,
        mesh=mesh,
        in_specs=(
            P(("row", "col"), None),
            P("col", "row"),
            P("row"),
            P("row", "col"),
            P("row", "col"),
            P("row", "col"),
            P("col", "row"),
            P("row"),
            P("row", "col"),
            P("row", "col"),
            P("col", "row"),
        ),
        out_specs=P(("row", "col"), None),
        check_vma=False,
    )
```
